32 devices in a mesh: study: 2 (over y), zslab: 4 (over x, core), frame: 4 (over z).
Axes of the slice: x: 2, y: 2, z: 4, core: 2. Of those that a mesh axis runs over, the one named last changes fastest.
Arguments:
- alpha: float32 [32, 64, 2048], P(('study', 'frame'), 'zslab'), parts along dimension 0, may hold values from 0.2 to 2
- measured: float32 [32, 64, 2048], P(('study', 'frame'), 'zslab'), parts along dimension 0, may hold values from 2 to 20
- background: float32 [32, 64, 2048], P(('study', 'frame'), 'zslab'), parts along dimension 0, may hold values from 1 to 4
- norm_image: float32 [32, 64, 2048], P(('study', 'frame'), 'zslab'), parts along dimension 0, may hold values from 3 to 12
- temporal: float32 [16, 16], replicated
- axial: float32 [64, 64], replicated, may hold values from 0 to 3.2, as said below
- kernel: bfloat16 [6144, 128, 128], P(('study', 'zslab', 'frame')), parts along dimension 0
- rows: int32 [6144], P(('study', 'zslab', 'frame')), parts along dimension 0, may hold values from 0 to 1023, as said below
- cols: int32 [6144], P(('study', 'zslab', 'frame')), parts along dimension 0, may hold values from 0 to 1023, as said below
- counts: int32 [32], P(('study', 'zslab', 'frame')), parts along dimension 0, may hold values from 64 to 192, as said below
Outputs:
- alpha_next: float32 [32, 64, 2048], P(('study', 'frame'), 'zslab'), parts along dimension 0
The draws below stay inside these ranges and needn't reach their ends.
There are 2 independent parts, one for each index of `study`. The reference program is written for one: setup_inputs(seed, part) draws one part's arguments, and reference() takes and returns one part's arrays. A program takes and returns all parts, laid end to end along the dimension named above; an argument that names none is the same for every part. Nothing has to cross between parts.
Inputs may be any that keep to these rules, and one draw needn't show every extreme that they name: Slots come in aligned runs of 192, one run for each device of zslab+frame in order, zslab slowest. A block row is plane * 16 + transaxial block; the rows of run d lie in the planes d // 4 * 16 to that + 15 and the transaxial blocks d % 4 * 4 to that + 3, appear in increasing order, and each of them has 1 to 3 live slots. `cols`: A live slot's column block has the transaxial block of its row and a plane at most one away from the row's plane. Slots that are not live repeat the run's first block row as row and column. counts[d] is the number of live slots of run d; they are the first slots of the run. In every draw one run is full. axial[z, y] is zero where |z - y| > 8.
All inputs are finite; a program needn't handle non-finite values.
Results may differ from the reference program's by a relative error of at most 0.0011.
Values may be sent and summed in bfloat16 or wider, within the bound.
A program may use at most 64 MiB of HBM per device.

```python
import math
import jax
import jax.numpy as jnp
from jax import lax

F = 16
BLOCK_VOXELS = 128
KROW = 3
AXR = 8
ZP = 16
BPD = 4
NZ = 64
PB = 16
PW = 2048
KCAP = 192
DEVS = 16
KERNEL_SLOTS = 3072
N_FRAME = 4


def slot_layout(key):
    row_count = ZP * BPD
    base = jax.random.fold_in(key, 7)
    key_count, key_full = jax.random.split(base)
    per_row = jax.random.randint(key_count, (DEVS, row_count), 1, KROW + 1)
    full_device = jax.random.randint(key_full, (), 0, DEVS)
    device_ids = jnp.arange(DEVS, dtype=jnp.int32)[:, None]
    per_row = jnp.where(device_ids == full_device, KROW, per_row)
    row_ends = jnp.cumsum(per_row, axis=1)
    row_starts = row_ends - per_row
    slot_ids = jnp.arange(KCAP, dtype=jnp.int32)
    row_of_slot = jnp.sum((row_starts[:, None, :] <= slot_ids[None, :, None]).astype(jnp.int32), axis=2) - 1
    row_of_slot = jnp.clip(row_of_slot, 0, row_count - 1)
    slot_in_row = slot_ids[None, :] - jnp.take_along_axis(row_starts, row_of_slot, axis=1)
    live_count = row_ends[:, -1]
    live_slot = slot_ids[None, :] < live_count[:, None]
    row_of_slot = jnp.where(live_slot, row_of_slot, 0)
    slot_in_row = jnp.where(live_slot, slot_in_row, 0)
    plane_local = row_of_slot // BPD
    block_local = row_of_slot % BPD
    row_plane = device_ids // N_FRAME * ZP + plane_local
    row_block = device_ids % N_FRAME * BPD + block_local
    plane_step = (1 - 2 * (slot_in_row % 2)) * ((slot_in_row + 1) // 2)
    col_plane = jnp.clip(row_plane + plane_step, 0, NZ - 1)
    row_ids = (row_plane * PB + row_block).reshape(-1).astype(jnp.int32)
    col_ids = (col_plane * PB + row_block).reshape(-1).astype(jnp.int32)
    return (row_ids, col_ids, live_count.astype(jnp.int32))


def draw_rows(key, part):
    return slot_layout(key)[0]


def draw_cols(key, part):
    return slot_layout(key)[1]


def draw_counts(key, part):
    return slot_layout(key)[2]


def draw_kernel(key, part):
    row_ids, col_ids, live_count = slot_layout(key)
    key_offdiagonal, key_diagonal, key_neighbor = jax.random.split(jax.random.fold_in(key, 11), 3)
    coarse_portion = jax.random.uniform(key_offdiagonal, (KERNEL_SLOTS, BLOCK_VOXELS, BLOCK_VOXELS), jnp.float32, 0.0, 1.0) / BLOCK_VOXELS
    own_diagonal = jax.random.uniform(key_diagonal, (KERNEL_SLOTS, BLOCK_VOXELS), jnp.float32, 0.5, 1.0)
    neighbor_diagonal = jax.random.uniform(key_neighbor, (KERNEL_SLOTS, BLOCK_VOXELS), jnp.float32, 0.2, 0.5)
    self_mask = (row_ids == col_ids)[:, None]
    diag_part = jnp.where(self_mask, own_diagonal, neighbor_diagonal)
    identity = jnp.eye(BLOCK_VOXELS, dtype=jnp.float32)
    return (coarse_portion + identity[None, :, :] * diag_part[:, :, None]).astype(jnp.bfloat16)


def draw_temporal(key, part):
    frame_ids = jnp.arange(F, dtype=jnp.float32)
    distance = jnp.abs(frame_ids[:, None] - frame_ids[None, :])
    coarse_portion = jax.random.uniform(key, (F, F), jnp.float32, 0.2, 1.0)
    return 0.5 * jnp.eye(F, dtype=jnp.float32) + coarse_portion * jnp.exp(-distance / 4.0) / 4.0


def draw_axial(key, part):
    plane_ids = jnp.arange(NZ, dtype=jnp.float32)
    distance = jnp.abs(plane_ids[:, None] - plane_ids[None, :])
    key_rough, key_diagonal = jax.random.split(key)
    coarse_portion = jax.random.uniform(key_rough, (NZ, NZ), jnp.float32, 0.5, 1.5)
    diag_part = jax.random.uniform(key_diagonal, (NZ,), jnp.float32, 0.5, 1.0)
    scaled = distance / AXR
    inside = (distance <= AXR).astype(jnp.float32)
    band = coarse_portion * jnp.exp(-scaled * scaled) * inside / AXR
    return band + jnp.eye(NZ, dtype=jnp.float32) * diag_part[None, :]


def block_scale(rng, shape, pieces, smallest, high):
    def one(dim, blocks):
        heights = jax.random.uniform(jax.random.fold_in(jax.random.fold_in(rng, 6), dim), (blocks,), jnp.float32, smallest / len(pieces), high / len(pieces))
        return jnp.repeat(jnp.exp(heights), shape[dim] // blocks).reshape((-1,) + (1,) * (len(shape) - dim - 1))

    factor_of = one(*pieces[0])
    for cut in pieces[1:]:
        factor_of = factor_of * one(*cut)
    return factor_of


def setup_inputs(seed: int = 0, part: int = 0) -> dict:
    splits = jax.random.split(jax.random.key(seed), 11)
    part_splits = jax.random.split(jax.random.fold_in(splits[10], part), 11)
    return {
        "alpha": jnp.clip(jnp.exp(math.log(2.0) - 2.3025851 * jax.random.uniform(part_splits[0], (F, NZ, PW), jnp.float32) ** block_scale(part_splits[0], (F, NZ, PW), ((0, 4), (1, 4)), -0.2, 0.2)), 0.2, 2.0),
        "measured": jnp.clip(jnp.exp(math.log(20.0) - 2.3025851 * jax.random.uniform(part_splits[1], (F, NZ, PW), jnp.float32) ** block_scale(part_splits[1], (F, NZ, PW), ((0, 4), (1, 4)), -0.2, 0.2)), 2.0, 20.0),
        "background": jnp.clip(jnp.exp(math.log(4.0) - 1.3862944 * jax.random.uniform(part_splits[2], (F, NZ, PW), jnp.float32) ** block_scale(part_splits[2], (F, NZ, PW), ((0, 4), (1, 4)), -0.2, 0.2)), 1.0, 4.0),
        "norm_image": jnp.clip(jnp.exp(math.log(12.0) - 1.3862944 * jax.random.uniform(part_splits[3], (F, NZ, PW), jnp.float32) ** block_scale(part_splits[3], (F, NZ, PW), ((0, 4), (1, 4)), -0.2, 0.2)), 3.0, 12.0),
        "temporal": draw_temporal(jax.random.fold_in(splits[10], 71), part),
        "axial": draw_axial(jax.random.fold_in(splits[10], 71), part),
        "kernel": draw_kernel(jax.random.fold_in(jax.random.fold_in(splits[10], part), 71), part),
        "rows": draw_rows(jax.random.fold_in(jax.random.fold_in(splits[10], part), 71), part),
        "cols": draw_cols(jax.random.fold_in(jax.random.fold_in(splits[10], part), 71), part),
        "counts": draw_counts(jax.random.fold_in(jax.random.fold_in(splits[10], part), 71), part),
    }


EXACT = lax.Precision.HIGHEST


def reference(alpha, measured, background, norm_image, temporal, axial, kernel, rows, cols, counts):
    lowered = alpha.astype(jnp.bfloat16).reshape(F, NZ * PB, BLOCK_VOXELS)
    slot_ids = jnp.arange(DEVS * KCAP, dtype=jnp.int32)
    live_mask = (slot_ids % KCAP < counts[slot_ids // KCAP]).astype(jnp.float32)
    kernel_runs = kernel.reshape(DEVS, KCAP, BLOCK_VOXELS, BLOCK_VOXELS)
    row_runs = rows.reshape(DEVS, KCAP)
    col_runs = cols.reshape(DEVS, KCAP)
    live_runs = live_mask.reshape(DEVS, KCAP)

    def forward_step(running, carried):
        kernel_blocks, row_ids, col_ids, weights = carried
        picked = lowered[:, col_ids, :].astype(jnp.float32)
        products = jnp.einsum("smn,fsn->fsm", kernel_blocks.astype(jnp.float32), picked, precision=EXACT)
        products = products * weights[None, :, None]
        return running.at[:, row_ids, :].add(products), None

    coef_image, _ = lax.scan(forward_step, jnp.zeros((F, NZ * PB, BLOCK_VOXELS), jnp.float32),
                             (kernel_runs, row_runs, col_runs, live_runs))
    coef_image = coef_image.reshape(F, NZ, PW)
    frame_image = jnp.einsum("fg,gzp->fzp", temporal, coef_image, precision=EXACT)
    expected = jnp.einsum("zy,fyp->fzp", axial, frame_image, precision=EXACT) + background
    ratios = measured / expected
    back_planes = jnp.einsum("zy,fzp->fyp", axial, ratios, precision=EXACT)
    back_frames = jnp.einsum("fg,fzp->gzp", temporal, back_planes, precision=EXACT)
    back_low = back_frames.astype(jnp.bfloat16).reshape(F, NZ * PB, BLOCK_VOXELS)

    def backward_step(running, carried):
        kernel_blocks, row_ids, col_ids, weights = carried
        picked = back_low[:, row_ids, :].astype(jnp.float32)
        products = jnp.einsum("smn,fsm->fsn", kernel_blocks.astype(jnp.float32), picked, precision=EXACT)
        products = products * weights[None, :, None]
        return running.at[:, col_ids, :].add(products), None

    back_coef, _ = lax.scan(backward_step, jnp.zeros((F, NZ * PB, BLOCK_VOXELS), jnp.float32),
                            (kernel_runs, row_runs, col_runs, live_runs))
    back_coef = back_coef.reshape(F, NZ, PW)
    return alpha * back_coef / norm_image
```

```python
import functools

import jax
import jax.numpy as jnp
from jax import lax
from jax.experimental import pallas as pl
from jax.experimental.pallas import tpu as pltpu
from jax.sharding import PartitionSpec as P

F32, BF16, I32 = jnp.float32, jnp.bfloat16, jnp.int32
MESH = pl.DeviceIdType.MESH
EXACT = lax.Precision.HIGHEST
REACH = 8
CHUNKS = 4
LEFT, RIGHT = 0, 1


def iota(shape, dim):
    return lax.broadcasted_iota(I32, shape, dim)


def hot(mask, dtype=F32):
    return jnp.where(mask, 1.0, 0.0).astype(dtype)


def exact(a, b):
    return jnp.dot(a, b, precision=EXACT, preferred_element_type=F32)


def exact_nt(a, b):
    return lax.dot_general(
        a, b, (((1,), (1,)), ((), ())), precision=EXACT, preferred_element_type=F32
    )


def em_kernel(
    sizes,
    alpha, measured, background, norm, temporal, axial, kernel,
    codes,
    out,
    outbox, inbox, image, coef, ratio, image_rim, coef_rim, ratio_rim, low, back,
    rim_out, rim, final_out, final_in, gathered,
    swap, forward_mix, backward_mix,
    a2a_send, a2a_recv, halo_send, halo_recv,
):
    ways, slabs, own, planes, tile, slots = sizes
    frames = ways * own
    width = tile // CHUNKS
    edge = 128
    per_chunk = width // edge
    tiles = tile // edge
    tiles_all = tiles * ways
    span = REACH * frames
    cells = planes * frames
    me = lax.axis_index("frame")
    slab = lax.axis_index("zslab")
    first = slab * planes
    beside = (lax.rem(slab + slabs - 1, slabs), lax.rem(slab + 1, slabs))

    def a2a(kind, c, o):
        if kind < 3:
            src, dst = outbox.at[kind, c, o - 1], inbox.at[kind, c, o]
        else:
            src, dst = final_out.at[c, o], final_in.at[c, o]
        return pltpu.make_async_remote_copy(
            src_ref=src, dst_ref=dst,
            send_sem=a2a_send.at[kind, c, o - 1], recv_sem=a2a_recv.at[kind, c, o - 1],
            device_id={"frame": lax.rem(me + o, ways)}, device_id_type=MESH,
        )

    def halo(kind, c, side):
        if kind == 0:
            src, dst = image.at[c, (1, planes)[side]], image_rim
        elif kind == 1:
            src, dst = coef.at[c, pl.ds((0, cells - span)[side], span)], coef_rim
        elif kind == 2:
            src, dst = ratio.at[c, pl.ds((0, cells - span)[side], span)], ratio_rim
        else:
            src, dst = rim_out.at[c, side], rim
        return pltpu.make_async_remote_copy(
            src_ref=src, dst_ref=dst.at[c, 1 - side],
            send_sem=halo_send.at[kind, c, side], recv_sem=halo_recv.at[kind, c, side],
            device_id={"zslab": beside[side]}, device_id_type=MESH,
        )

    def halo_start(kind, c):
        for side in (LEFT, RIGHT):
            halo(kind, c, side).start()

    def halo_wait(kind, c):
        for side in (LEFT, RIGHT):
            halo(kind, c, side).wait_recv()

    def fill(kind, source):
        for c in range(CHUNKS):
            for o in range(ways):
                lanes = pl.ds(pl.multiple_of(lax.rem(me + o, ways) * tile + c * width, edge), width)
                part = source[:, :, lanes].reshape(own * planes, width).astype(BF16)
                if o == 0:
                    inbox[kind, c, 0] = part
                else:
                    outbox[kind, c, o - 1] = part

    fill(0, alpha)
    fill(1, measured)
    fill(2, background)
    barrier = pltpu.get_barrier_semaphore()
    for o in range(1, ways):
        pl.semaphore_signal(
            barrier, inc=1, device_id={"frame": lax.rem(me + o, ways)}, device_id_type=MESH
        )
    for side in (LEFT, RIGHT):
        pl.semaphore_signal(
            barrier, inc=1, device_id={"zslab": beside[side]}, device_id_type=MESH
        )
    pl.semaphore_wait(barrier, ways + 1)
    for kinds in ((0,), (1, 2)):
        for c in range(CHUNKS):
            for kind in kinds:
                for o in range(1, ways):
                    a2a(kind, c, o).start()

    def frame_in(p):
        return lax.rem(me + ways - p // own, ways) * own + p % own

    def frame_out(p):
        return lax.rem(me + p // own, ways) * own + p % own

    row, column = iota((cells, cells), 0), iota((cells, cells), 1)
    swap[0] = hot(
        column % planes * frames + frame_in(column // planes) == row, BF16
    )
    swap[1] = hot(
        row % planes * frames + frame_out(row // planes) == column, BF16
    )

    def plane_at(k):
        return first + jnp.where(
            k < planes, k, jnp.where(k < planes + REACH, k - planes - REACH, k - REACH)
        )

    all_planes = axial.shape[0]
    wide = (planes + 2 * REACH) * frames
    halves = planes // REACH
    spread = hot(iota((all_planes, wide), 0) == plane_at(iota((all_planes, wide), 1) // frames))
    axial_wide = exact(axial[pl.ds(pl.multiple_of(first, REACH), planes), :], spread)
    time_wide = exact(temporal[...], hot(iota((frames, wide), 0) == iota((frames, wide), 1) % frames))
    time_rows = exact(
        hot(iota((span, frames), 1) == frame_in(iota((span, frames), 0) // REACH)), time_wide
    )
    for h in range(halves):
        axial_rows = jnp.broadcast_to(
            axial_wide[h * REACH:(h + 1) * REACH][None], (frames, REACH, wide)
        ).reshape(span, wide)
        forward_mix[h * span:(h + 1) * span] = (axial_rows * time_rows).astype(BF16)

    lane = iota((all_planes, wide), 1)
    spread = hot(
        iota((all_planes, wide), 0) == plane_at(lane // span * REACH + lane % REACH)
    )
    pick = hot(iota((planes, all_planes), 1) == first + iota((planes, all_planes), 0))
    axial_wide = exact(exact_nt(pick, axial[...]), spread)
    same = hot(iota((frames, frames), 0) == iota((frames, frames), 1))
    time_wide = exact(
        exact_nt(same, temporal[...]),
        hot(iota((frames, wide), 0) == frame_in(iota((frames, wide), 1) // REACH % frames)),
    )
    axial_rows = exact(hot(iota((cells, planes), 1) == iota((cells, planes), 0) // frames), axial_wide)
    time_rows = jnp.broadcast_to(time_wide[None], (planes, frames, wide)).reshape(cells, wide)
    backward_mix[...] = (axial_rows * time_rows).astype(BF16)

    def stage_image(c):
        for o in range(1, ways):
            a2a(0, c, o).wait_recv()
        moved = jnp.dot(swap[0], inbox[0, c].reshape(cells, width), preferred_element_type=F32)
        image[c, 1:planes + 1] = moved.astype(BF16).reshape(planes, frames, width)
        halo_start(0, c)

    group = 4

    def slot_of(r, j):
        return 3 * r + j, codes[3 * r + j]

    def weight(code, value):
        return jnp.where(code == value, 1.0, 0.0).astype(F32)

    def stage_forward(c):
        halo_wait(0, c)
        image[c, 0] = image_rim[c, LEFT]
        image[c, planes + 1] = image_rim[c, RIGHT]
        for b in range(per_chunk):
            lanes = slice(b * edge, (b + 1) * edge)

            def some_planes(step, carry):
                for u in range(group):
                    z = step * group + u
                    r = z * tiles + c * per_chunk + b
                    near = [image[c, z + d, :, lanes].astype(F32) for d in range(3)]
                    total = None
                    for j in range(3):
                        slot, code = slot_of(r, j)
                        picked = sum(near[d] * weight(code, d + 1) for d in range(3)).astype(BF16)
                        term = lax.dot_general(
                            picked, kernel[slot], (((1,), (1,)), ((), ())),
                            preferred_element_type=F32,
                        )
                        total = term if total is None else total + term
                    at = pl.multiple_of(z * frames, frames)
                    gathered[pl.ds(at, frames), lanes] = total.astype(BF16)
                return carry

            lax.fori_loop(0, planes // group, some_planes, 0)
        coef[c] = gathered[...]
        halo_start(1, c)

    def by_half(box, c, h):
        cube = box[c].astype(F32).reshape(frames, halves, REACH, width)
        return cube[:, h].reshape(span, width)

    def stage_ratio(c):
        for kind in (1, 2):
            for o in range(1, ways):
                a2a(kind, c, o).wait_recv()
        projected = jnp.dot(forward_mix[:, :cells], coef[c], preferred_element_type=F32)
        halo_wait(1, c)
        projected = projected + jnp.dot(
            forward_mix[:, cells:], coef_rim[c].reshape(2 * span, width), preferred_element_type=F32
        )
        for h in range(halves):
            expected = projected[h * span:(h + 1) * span] + by_half(inbox.at[2], c, h)
            ratio[c, h * span:(h + 1) * span] = (
                by_half(inbox.at[1], c, h) / expected
            ).astype(BF16)
        halo_start(2, c)

    def stage_back(c):
        mixed = jnp.dot(backward_mix[:, :cells], ratio[c], preferred_element_type=F32)
        halo_wait(2, c)
        mixed = mixed + jnp.dot(
            backward_mix[:, cells:], ratio_rim[c].reshape(2 * span, width), preferred_element_type=F32
        )
        low[c] = mixed.astype(BF16).reshape(planes, frames, width)
        back[c] = jnp.zeros((planes + 2, frames, width), F32)
        for b in range(per_chunk):
            lanes = slice(b * edge, (b + 1) * edge)

            def some_planes(step, carry):
                sums = [jnp.zeros((frames, edge), F32) for _ in range(group + 2)]
                for u in range(group):
                    z = step * group + u
                    r = z * tiles + c * per_chunk + b
                    values = low[c, z, :, lanes]
                    for j in range(3):
                        slot, code = slot_of(r, j)
                        term = jnp.dot(values, kernel[slot], preferred_element_type=F32)
                        for d in range(3):
                            sums[u + d] = sums[u + d] + term * weight(code, d + 1)
                for u in range(group + 2):
                    back[c, step * group + u, :, lanes] += sums[u]
                return carry

            lax.fori_loop(0, planes // group, some_planes, 0)
        rim_out[c, LEFT] = back[c, 0]
        rim_out[c, RIGHT] = back[c, planes + 1]
        halo_start(3, c)

    def stage_send(c):
        halo_wait(3, c)
        back[c, 1] += rim[c, 0]
        back[c, planes] += rim[c, 1]
        whole = back[c, 1:planes + 1].reshape(cells, width)
        high = whole.astype(BF16)
        rest = (whole - high.astype(F32)).astype(BF16)
        moved = jnp.dot(swap[1], high, preferred_element_type=F32) + jnp.dot(
            swap[1], rest, preferred_element_type=F32
        )
        moved = moved.reshape(ways, own * planes, width)
        final_out[c] = moved
        for o in range(1, ways):
            a2a(3, c, o).start()

    def stage_out(c):
        for o in range(ways):
            if o > 0:
                a2a(3, c, o).wait_recv()
            source = lax.rem(me + ways - o, ways)
            lanes = pl.ds(pl.multiple_of(source * tile + c * width, edge), width)
            values = (final_in if o else final_out)[c, o].reshape(own, planes, width)
            out[:, :, lanes] = alpha[:, :, lanes] * values / norm[:, :, lanes]

    stages = (stage_image, stage_forward, stage_ratio, stage_back, stage_send, stage_out)
    for t in range(CHUNKS + len(stages) - 1):
        for s, stage in enumerate(stages):
            if 0 <= t - s < CHUNKS:
                stage(t - s)

    for c in range(CHUNKS):
        for kind in range(4):
            for o in range(1, ways):
                a2a(kind, c, o).wait_send()
            for side in (LEFT, RIGHT):
                halo(kind, c, side).wait_send()


def on_device(alpha, measured, background, norm_image, temporal, axial, kernel, rows, cols, counts):
    own, planes, row_width = alpha.shape
    ways, slabs = lax.axis_size("frame"), lax.axis_size("zslab")
    slots, edge, _ = kernel.shape
    frames = ways * own
    tile = row_width // ways
    width = tile // CHUNKS
    cells = planes * frames
    wide = (planes + 2 * REACH) * frames
    tiles_all, tiles = row_width // edge, tile // edge
    first = lax.axis_index("zslab") * planes
    here = lax.axis_index("frame") * tiles
    local_rows = (rows // tiles_all - first) * tiles + rows % tiles_all - here
    step = cols // tiles_all - rows // tiles_all
    live = jnp.arange(slots, dtype=I32) < counts[0]
    local_rows = jnp.where(live, local_rows, planes * tiles)
    order = jnp.arange(planes * tiles, dtype=I32)
    starts = jnp.sum((local_rows[None, :] < order[:, None]).astype(I32), axis=1)
    places = starts[:, None] + jnp.arange(3, dtype=I32)[None, :]
    chosen = places[:, :, None] == jnp.arange(slots, dtype=I32)[None, None, :]
    mine = chosen & (local_rows[None, None, :] == order[:, None, None])
    codes = jnp.sum(jnp.where(mine, step + 2, 0), axis=2).reshape(-1)
    ordered = jnp.take(kernel, jnp.minimum(places, slots - 1).reshape(-1), axis=0, mode="clip")
    sizes = (ways, slabs, own, planes, tile, slots)
    vmem = pl.BlockSpec(memory_space=pltpu.VMEM)
    smem = pl.BlockSpec(memory_space=pltpu.SMEM)
    box = (CHUNKS, ways, own * planes, width)
    return pl.pallas_call(
        functools.partial(em_kernel, sizes),
        out_shape=jax.ShapeDtypeStruct(alpha.shape, F32),
        in_specs=[vmem] * 7 + [smem],
        out_specs=vmem,
        scratch_shapes=[
            pltpu.VMEM((3, CHUNKS, ways - 1, own * planes, width), BF16),
            pltpu.VMEM((3,) + box, BF16),
            pltpu.VMEM((CHUNKS, planes + 2, frames, width), BF16),
            pltpu.VMEM((CHUNKS, cells, width), BF16),
            pltpu.VMEM((CHUNKS, cells, width), BF16),
            pltpu.VMEM((CHUNKS, 2, frames, width), BF16),
            pltpu.VMEM((CHUNKS, 2, REACH * frames, width), BF16),
            pltpu.VMEM((CHUNKS, 2, REACH * frames, width), BF16),
            pltpu.VMEM((CHUNKS, planes, frames, width), BF16),
            pltpu.VMEM((CHUNKS, planes + 2, frames, width), F32),
            pltpu.VMEM((CHUNKS, 2, frames, width), F32),
            pltpu.VMEM((CHUNKS, 2, frames, width), F32),
            pltpu.VMEM(box, F32),
            pltpu.VMEM(box, F32),
            pltpu.VMEM((cells, width), BF16),
            pltpu.VMEM((2, cells, cells), BF16),
            pltpu.VMEM((cells, wide), BF16),
            pltpu.VMEM((cells, wide), BF16),
            pltpu.SemaphoreType.DMA((4, CHUNKS, ways - 1)),
            pltpu.SemaphoreType.DMA((4, CHUNKS, ways - 1)),
            pltpu.SemaphoreType.DMA((4, CHUNKS, 2)),
            pltpu.SemaphoreType.DMA((4, CHUNKS, 2)),
        ],
        compiler_params=pltpu.CompilerParams(
            collective_id=0, has_side_effects=True, vmem_limit_bytes=48 * 1024 * 1024
        ),
        cost_estimate=pl.CostEstimate(
            flops=8 * frames * slots * edge * edge, bytes_accessed=2 * slots * edge * edge,
            transcendentals=0,
        ),
    )(alpha, measured, background, norm_image, temporal, axial, ordered, codes)


def solution(mesh):
    placed = (
        P(("study", "frame"), "zslab", None),
        P(("study", "frame"), "zslab", None),
        P(("study", "frame"), "zslab", None),
        P(("study", "frame"), "zslab", None),
        P(),
        P(),
        P(("study", "zslab", "frame"), None, None),
        P(("study", "zslab", "frame")),
        P(("study", "zslab", "frame")),
        P(("study", "zslab", "frame")),
    )
    return jax.shard_map(
        on_device,
        mesh=mesh,
        in_specs=placed,
        out_specs=P(("study", "frame"), "zslab", None),
        check_vma=False,
    )
```

```python
import functools

import jax
import jax.numpy as jnp
from jax import lax
from jax.experimental import pallas as pl
from jax.experimental.pallas import tpu as pltpu
from jax.sharding import PartitionSpec as P

F32, BF16, I32 = jnp.float32, jnp.bfloat16, jnp.int32
MESH = pl.DeviceIdType.MESH
EXACT = lax.Precision.HIGHEST
REACH = 8
CHUNKS = 4
LEFT, RIGHT = 0, 1


def iota(shape, dim):
    return lax.broadcasted_iota(I32, shape, dim)


def hot(mask, dtype=F32):
    return jnp.where(mask, 1.0, 0.0).astype(dtype)


def exact(a, b):
    return jnp.dot(a, b, precision=EXACT, preferred_element_type=F32)


def exact_nt(a, b):
    return lax.dot_general(
        a, b, (((1,), (1,)), ((), ())), precision=EXACT, preferred_element_type=F32
    )


def em_kernel(
    sizes,
    alpha, measured, background, norm, temporal, axial, kernel,
    codes, chosen,
    out,
    outbox, inbox, image, coef, ratio, image_rim, coef_rim, ratio_rim, low, back,
    rim_out, rim, final_out, final_in, gathered,
    swap, forward_mix, backward_mix,
    a2a_send, a2a_recv, halo_send, halo_recv,
):
    ways, slabs, own, planes, tile, slots = sizes
    frames = ways * own
    width = tile // CHUNKS
    edge = 128
    per_chunk = width // edge
    tiles = tile // edge
    tiles_all = tiles * ways
    span = REACH * frames
    cells = planes * frames
    me = lax.axis_index("frame")
    slab = lax.axis_index("zslab")
    first = slab * planes
    beside = (lax.rem(slab + slabs - 1, slabs), lax.rem(slab + 1, slabs))

    def a2a(kind, c, o):
        if kind < 3:
            src, dst = outbox.at[kind, c, o - 1], inbox.at[kind, c, o]
        else:
            src, dst = final_out.at[c, o], final_in.at[c, o]
        return pltpu.make_async_remote_copy(
            src_ref=src, dst_ref=dst,
            send_sem=a2a_send.at[kind, c, o - 1], recv_sem=a2a_recv.at[kind, c, o - 1],
            device_id={"frame": lax.rem(me + o, ways)}, device_id_type=MESH,
        )

    def halo(kind, c, side):
        if kind == 0:
            src, dst = image.at[c, (1, planes)[side]], image_rim
        elif kind == 1:
            src, dst = coef.at[c, pl.ds((0, cells - span)[side], span)], coef_rim
        elif kind == 2:
            src, dst = ratio.at[c, pl.ds((0, cells - span)[side], span)], ratio_rim
        else:
            src, dst = rim_out.at[c, side], rim
        return pltpu.make_async_remote_copy(
            src_ref=src, dst_ref=dst.at[c, 1 - side],
            send_sem=halo_send.at[kind, c, side], recv_sem=halo_recv.at[kind, c, side],
            device_id={"zslab": beside[side]}, device_id_type=MESH,
        )

    def halo_start(kind, c):
        for side in (LEFT, RIGHT):
            halo(kind, c, side).start()

    def halo_wait(kind, c):
        for side in (LEFT, RIGHT):
            halo(kind, c, side).wait_recv()

    def fill(kind, source):
        for c in range(CHUNKS):
            for o in range(ways):
                lanes = pl.ds(pl.multiple_of(lax.rem(me + o, ways) * tile + c * width, edge), width)
                part = source[:, :, lanes].reshape(own * planes, width).astype(BF16)
                if o == 0:
                    inbox[kind, c, 0] = part
                else:
                    outbox[kind, c, o - 1] = part

    fill(0, alpha)
    fill(1, measured)
    fill(2, background)
    barrier = pltpu.get_barrier_semaphore()
    for o in range(1, ways):
        pl.semaphore_signal(
            barrier, inc=1, device_id={"frame": lax.rem(me + o, ways)}, device_id_type=MESH
        )
    for side in (LEFT, RIGHT):
        pl.semaphore_signal(
            barrier, inc=1, device_id={"zslab": beside[side]}, device_id_type=MESH
        )
    pl.semaphore_wait(barrier, ways + 1)
    for kinds in ((0,), (1, 2)):
        for c in range(CHUNKS):
            for kind in kinds:
                for o in range(1, ways):
                    a2a(kind, c, o).start()

    def frame_in(p):
        return lax.rem(me + ways - p // own, ways) * own + p % own

    def frame_out(p):
        return lax.rem(me + p // own, ways) * own + p % own

    row, column = iota((cells, cells), 0), iota((cells, cells), 1)
    swap[0] = hot(
        column % planes * frames + frame_in(column // planes) == row, BF16
    )
    swap[1] = hot(
        row % planes * frames + frame_out(row // planes) == column, BF16
    )

    def plane_at(k):
        return first + jnp.where(
            k < planes, k, jnp.where(k < planes + REACH, k - planes - REACH, k - REACH)
        )

    all_planes = axial.shape[0]
    wide = (planes + 2 * REACH) * frames
    halves = planes // REACH
    spread = hot(iota((all_planes, wide), 0) == plane_at(iota((all_planes, wide), 1) // frames))
    axial_wide = exact(axial[pl.ds(pl.multiple_of(first, REACH), planes), :], spread)
    time_wide = exact(temporal[...], hot(iota((frames, wide), 0) == iota((frames, wide), 1) % frames))
    time_rows = exact(
        hot(iota((span, frames), 1) == frame_in(iota((span, frames), 0) // REACH)), time_wide
    )
    for h in range(halves):
        axial_rows = jnp.broadcast_to(
            axial_wide[h * REACH:(h + 1) * REACH][None], (frames, REACH, wide)
        ).reshape(span, wide)
        forward_mix[h * span:(h + 1) * span] = (axial_rows * time_rows).astype(BF16)

    lane = iota((all_planes, wide), 1)
    spread = hot(
        iota((all_planes, wide), 0) == plane_at(lane // span * REACH + lane % REACH)
    )
    pick = hot(iota((planes, all_planes), 1) == first + iota((planes, all_planes), 0))
    axial_wide = exact(exact_nt(pick, axial[...]), spread)
    same = hot(iota((frames, frames), 0) == iota((frames, frames), 1))
    time_wide = exact(
        exact_nt(same, temporal[...]),
        hot(iota((frames, wide), 0) == frame_in(iota((frames, wide), 1) // REACH % frames)),
    )
    axial_rows = exact(hot(iota((cells, planes), 1) == iota((cells, planes), 0) // frames), axial_wide)
    time_rows = jnp.broadcast_to(time_wide[None], (planes, frames, wide)).reshape(cells, wide)
    backward_mix[...] = (axial_rows * time_rows).astype(BF16)

    def stage_image(c):
        for o in range(1, ways):
            a2a(0, c, o).wait_recv()
        moved = jnp.dot(swap[0], inbox[0, c].reshape(cells, width), preferred_element_type=F32)
        image[c, 1:planes + 1] = moved.astype(BF16).reshape(planes, frames, width)
        halo_start(0, c)

    group = 4

    def slot_of(r, j):
        return chosen[3 * r + j], codes[3 * r + j]

    def weight(code, value):
        return jnp.where(code == value, 1.0, 0.0).astype(F32)

    def stage_forward(c):
        halo_wait(0, c)
        image[c, 0] = image_rim[c, LEFT]
        image[c, planes + 1] = image_rim[c, RIGHT]
        for b in range(per_chunk):
            lanes = slice(b * edge, (b + 1) * edge)

            def some_planes(step, carry):
                for u in range(group):
                    z = step * group + u
                    r = z * tiles + c * per_chunk + b
                    near = [image[c, z + d, :, lanes].astype(F32) for d in range(3)]
                    total = None
                    for j in range(3):
                        slot, code = slot_of(r, j)
                        picked = sum(near[d] * weight(code, d + 1) for d in range(3)).astype(BF16)
                        term = lax.dot_general(
                            picked, kernel[slot], (((1,), (1,)), ((), ())),
                            preferred_element_type=F32,
                        )
                        total = term if total is None else total + term
                    at = pl.multiple_of(z * frames, frames)
                    gathered[pl.ds(at, frames), lanes] = total.astype(BF16)
                return carry

            lax.fori_loop(0, planes // group, some_planes, 0)
        coef[c] = gathered[...]
        halo_start(1, c)

    def by_half(box, c, h):
        cube = box[c].astype(F32).reshape(frames, halves, REACH, width)
        return cube[:, h].reshape(span, width)

    def stage_ratio(c):
        for kind in (1, 2):
            for o in range(1, ways):
                a2a(kind, c, o).wait_recv()
        projected = jnp.dot(forward_mix[:, :cells], coef[c], preferred_element_type=F32)
        halo_wait(1, c)
        projected = projected + jnp.dot(
            forward_mix[:, cells:], coef_rim[c].reshape(2 * span, width), preferred_element_type=F32
        )
        for h in range(halves):
            expected = projected[h * span:(h + 1) * span] + by_half(inbox.at[2], c, h)
            ratio[c, h * span:(h + 1) * span] = (
                by_half(inbox.at[1], c, h) / expected
            ).astype(BF16)
        halo_start(2, c)

    def stage_back(c):
        mixed = jnp.dot(backward_mix[:, :cells], ratio[c], preferred_element_type=F32)
        halo_wait(2, c)
        mixed = mixed + jnp.dot(
            backward_mix[:, cells:], ratio_rim[c].reshape(2 * span, width), preferred_element_type=F32
        )
        low[c] = mixed.astype(BF16).reshape(planes, frames, width)
        back[c] = jnp.zeros((planes + 2, frames, width), F32)
        for b in range(per_chunk):
            lanes = slice(b * edge, (b + 1) * edge)

            def some_planes(step, carry):
                sums = [jnp.zeros((frames, edge), F32) for _ in range(group + 2)]
                for u in range(group):
                    z = step * group + u
                    r = z * tiles + c * per_chunk + b
                    values = low[c, z, :, lanes]
                    for j in range(3):
                        slot, code = slot_of(r, j)
                        term = jnp.dot(values, kernel[slot], preferred_element_type=F32)
                        for d in range(3):
                            sums[u + d] = sums[u + d] + term * weight(code, d + 1)
                for u in range(group + 2):
                    back[c, step * group + u, :, lanes] += sums[u]
                return carry

            lax.fori_loop(0, planes // group, some_planes, 0)
        rim_out[c, LEFT] = back[c, 0]
        rim_out[c, RIGHT] = back[c, planes + 1]
        halo_start(3, c)

    def stage_send(c):
        halo_wait(3, c)
        back[c, 1] += rim[c, 0]
        back[c, planes] += rim[c, 1]
        whole = back[c, 1:planes + 1].reshape(cells, width)
        high = whole.astype(BF16)
        rest = (whole - high.astype(F32)).astype(BF16)
        moved = jnp.dot(swap[1], high, preferred_element_type=F32) + jnp.dot(
            swap[1], rest, preferred_element_type=F32
        )
        moved = moved.reshape(ways, own * planes, width)
        final_out[c] = moved
        for o in range(1, ways):
            a2a(3, c, o).start()

    def stage_out(c):
        for o in range(ways):
            if o > 0:
                a2a(3, c, o).wait_recv()
            source = lax.rem(me + ways - o, ways)
            lanes = pl.ds(pl.multiple_of(source * tile + c * width, edge), width)
            values = (final_in if o else final_out)[c, o].reshape(own, planes, width)
            out[:, :, lanes] = alpha[:, :, lanes] * values / norm[:, :, lanes]

    stages = (stage_image, stage_forward, stage_ratio, stage_back, stage_send, stage_out)
    for t in range(CHUNKS + len(stages) - 1):
        for s, stage in enumerate(stages):
            if 0 <= t - s < CHUNKS:
                stage(t - s)

    for c in range(CHUNKS):
        for kind in range(4):
            for o in range(1, ways):
                a2a(kind, c, o).wait_send()
            for side in (LEFT, RIGHT):
                halo(kind, c, side).wait_send()


def on_device(alpha, measured, background, norm_image, temporal, axial, kernel, rows, cols, counts):
    own, planes, row_width = alpha.shape
    ways, slabs = lax.axis_size("frame"), lax.axis_size("zslab")
    slots, edge, _ = kernel.shape
    frames = ways * own
    tile = row_width // ways
    width = tile // CHUNKS
    cells = planes * frames
    wide = (planes + 2 * REACH) * frames
    tiles_all, tiles = row_width // edge, tile // edge
    first = lax.axis_index("zslab") * planes
    here = lax.axis_index("frame") * tiles
    local_rows = (rows // tiles_all - first) * tiles + rows % tiles_all - here
    step = cols // tiles_all - rows // tiles_all
    live = jnp.arange(slots, dtype=I32) < counts[0]
    local_rows = jnp.where(live, local_rows, planes * tiles)
    order = jnp.arange(planes * tiles, dtype=I32)
    starts = jnp.sum((local_rows[None, :] < order[:, None]).astype(I32), axis=1)
    places = starts[:, None] + jnp.arange(3, dtype=I32)[None, :]
    chosen = places[:, :, None] == jnp.arange(slots, dtype=I32)[None, None, :]
    mine = chosen & (local_rows[None, None, :] == order[:, None, None])
    codes = jnp.sum(jnp.where(mine, step + 2, 0), axis=2).reshape(-1)
    spots = jnp.minimum(places, slots - 1).reshape(-1)
    sizes = (ways, slabs, own, planes, tile, slots)
    vmem = pl.BlockSpec(memory_space=pltpu.VMEM)
    smem = pl.BlockSpec(memory_space=pltpu.SMEM)
    box = (CHUNKS, ways, own * planes, width)
    return pl.pallas_call(
        functools.partial(em_kernel, sizes),
        out_shape=jax.ShapeDtypeStruct(alpha.shape, F32),
        in_specs=[vmem] * 7 + [smem] * 2,
        out_specs=vmem,
        scratch_shapes=[
            pltpu.VMEM((3, CHUNKS, ways - 1, own * planes, width), BF16),
            pltpu.VMEM((3,) + box, BF16),
            pltpu.VMEM((CHUNKS, planes + 2, frames, width), BF16),
            pltpu.VMEM((CHUNKS, cells, width), BF16),
            pltpu.VMEM((CHUNKS, cells, width), BF16),
            pltpu.VMEM((CHUNKS, 2, frames, width), BF16),
            pltpu.VMEM((CHUNKS, 2, REACH * frames, width), BF16),
            pltpu.VMEM((CHUNKS, 2, REACH * frames, width), BF16),
            pltpu.VMEM((CHUNKS, planes, frames, width), BF16),
            pltpu.VMEM((CHUNKS, planes + 2, frames, width), F32),
            pltpu.VMEM((CHUNKS, 2, frames, width), F32),
            pltpu.VMEM((CHUNKS, 2, frames, width), F32),
            pltpu.VMEM(box, F32),
            pltpu.VMEM(box, F32),
            pltpu.VMEM((cells, width), BF16),
            pltpu.VMEM((2, cells, cells), BF16),
            pltpu.VMEM((cells, wide), BF16),
            pltpu.VMEM((cells, wide), BF16),
            pltpu.SemaphoreType.DMA((4, CHUNKS, ways - 1)),
            pltpu.SemaphoreType.DMA((4, CHUNKS, ways - 1)),
            pltpu.SemaphoreType.DMA((4, CHUNKS, 2)),
            pltpu.SemaphoreType.DMA((4, CHUNKS, 2)),
        ],
        compiler_params=pltpu.CompilerParams(
            collective_id=0, has_side_effects=True, vmem_limit_bytes=48 * 1024 * 1024
        ),
        cost_estimate=pl.CostEstimate(
            flops=8 * frames * slots * edge * edge, bytes_accessed=2 * slots * edge * edge,
            transcendentals=0,
        ),
    )(alpha, measured, background, norm_image, temporal, axial, kernel, codes, spots)


def solution(mesh):
    placed = (
        P(("study", "frame"), "zslab", None),
        P(("study", "frame"), "zslab", None),
        P(("study", "frame"), "zslab", None),
        P(("study", "frame"), "zslab", None),
        P(),
        P(),
        P(("study", "zslab", "frame"), None, None),
        P(("study", "zslab", "frame")),
        P(("study", "zslab", "frame")),
        P(("study", "zslab", "frame")),
    )
    return jax.shard_map(
        on_device,
        mesh=mesh,
        in_specs=placed,
        out_specs=P(("study", "frame"), "zslab", None),
        check_vma=False,
    )
```

```python
import functools

import jax
import jax.numpy as jnp
from jax import lax
from jax.experimental import pallas as pl
from jax.experimental.pallas import tpu as pltpu
from jax.sharding import PartitionSpec as P

F32, BF16, I32 = jnp.float32, jnp.bfloat16, jnp.int32
MESH = pl.DeviceIdType.MESH
EXACT = lax.Precision.HIGHEST
REACH = 8
CHUNKS = 4
LEFT, RIGHT = 0, 1


def iota(shape, dim):
    return lax.broadcasted_iota(I32, shape, dim)


def hot(mask, dtype=F32):
    return jnp.where(mask, 1.0, 0.0).astype(dtype)


def exact(a, b):
    return jnp.dot(a, b, precision=EXACT, preferred_element_type=F32)


def exact_nt(a, b):
    return lax.dot_general(
        a, b, (((1,), (1,)), ((), ())), precision=EXACT, preferred_element_type=F32
    )


def em_kernel(
    sizes,
    alpha_hbm, measured_hbm, background_hbm, norm_hbm, temporal, axial, kernel_hbm,
    codes, chosen,
    out,
    alpha, measured, background, norm, kernel,
    outbox, inbox, image, coef, ratio, image_rim, coef_rim, ratio_rim, low, back,
    rim_out, rim, final_out, final_in, gathered,
    swap, forward_mix, backward_mix,
    a2a_send, a2a_recv, halo_send, halo_recv, local_sem,
):
    ways, slabs, own, planes, tile, slots = sizes
    frames = ways * own
    width = tile // CHUNKS
    edge = 128
    per_chunk = width // edge
    tiles = tile // edge
    tiles_all = tiles * ways
    span = REACH * frames
    cells = planes * frames
    me = lax.axis_index("frame")
    slab = lax.axis_index("zslab")
    first = slab * planes
    beside = (lax.rem(slab + slabs - 1, slabs), lax.rem(slab + 1, slabs))

    def a2a(kind, c, o):
        if kind < 3:
            src, dst = outbox.at[kind, c, o - 1], inbox.at[kind, c, o]
        else:
            src, dst = final_out.at[c, o], final_in.at[c, o]
        return pltpu.make_async_remote_copy(
            src_ref=src, dst_ref=dst,
            send_sem=a2a_send.at[kind, c, o - 1], recv_sem=a2a_recv.at[kind, c, o - 1],
            device_id={"frame": lax.rem(me + o, ways)}, device_id_type=MESH,
        )

    def halo(kind, c, side):
        if kind == 0:
            src, dst = image.at[c, (1, planes)[side]], image_rim
        elif kind == 1:
            src, dst = coef.at[c, pl.ds((0, cells - span)[side], span)], coef_rim
        elif kind == 2:
            src, dst = ratio.at[c, pl.ds((0, cells - span)[side], span)], ratio_rim
        else:
            src, dst = rim_out.at[c, side], rim
        return pltpu.make_async_remote_copy(
            src_ref=src, dst_ref=dst.at[c, 1 - side],
            send_sem=halo_send.at[kind, c, side], recv_sem=halo_recv.at[kind, c, side],
            device_id={"zslab": beside[side]}, device_id_type=MESH,
        )

    def halo_start(kind, c):
        for side in (LEFT, RIGHT):
            halo(kind, c, side).start()

    def halo_wait(kind, c):
        for side in (LEFT, RIGHT):
            halo(kind, c, side).wait_recv()

    def fill(kind, source):
        for c in range(CHUNKS):
            for o in range(ways):
                lanes = pl.ds(pl.multiple_of(lax.rem(me + o, ways) * tile + c * width, edge), width)
                part = source[:, :, lanes].reshape(own * planes, width).astype(BF16)
                if o == 0:
                    inbox[kind, c, 0] = part
                else:
                    outbox[kind, c, o - 1] = part

    local = [
        pltpu.make_async_copy(src, dst, local_sem.at[i])
        for i, (src, dst) in enumerate(
            ((alpha_hbm, alpha), (measured_hbm, measured), (background_hbm, background),
             (kernel_hbm, kernel), (norm_hbm, norm))
        )
    ]
    for copy in local:
        copy.start()
    for kind, source in enumerate((alpha, measured, background)):
        local[kind].wait()
        fill(kind, source)
    barrier = pltpu.get_barrier_semaphore()
    for o in range(1, ways):
        pl.semaphore_signal(
            barrier, inc=1, device_id={"frame": lax.rem(me + o, ways)}, device_id_type=MESH
        )
    for side in (LEFT, RIGHT):
        pl.semaphore_signal(
            barrier, inc=1, device_id={"zslab": beside[side]}, device_id_type=MESH
        )
    pl.semaphore_wait(barrier, ways + 1)
    for kinds in ((0,), (1, 2)):
        for c in range(CHUNKS):
            for kind in kinds:
                for o in range(1, ways):
                    a2a(kind, c, o).start()

    def frame_in(p):
        return lax.rem(me + ways - p // own, ways) * own + p % own

    def frame_out(p):
        return lax.rem(me + p // own, ways) * own + p % own

    row, column = iota((cells, cells), 0), iota((cells, cells), 1)
    swap[0] = hot(
        column % planes * frames + frame_in(column // planes) == row, BF16
    )
    swap[1] = hot(
        row % planes * frames + frame_out(row // planes) == column, BF16
    )

    def plane_at(k):
        return first + jnp.where(
            k < planes, k, jnp.where(k < planes + REACH, k - planes - REACH, k - REACH)
        )

    all_planes = axial.shape[0]
    wide = (planes + 2 * REACH) * frames
    halves = planes // REACH
    spread = hot(iota((all_planes, wide), 0) == plane_at(iota((all_planes, wide), 1) // frames))
    axial_wide = exact(axial[pl.ds(pl.multiple_of(first, REACH), planes), :], spread)
    time_wide = exact(temporal[...], hot(iota((frames, wide), 0) == iota((frames, wide), 1) % frames))
    time_rows = exact(
        hot(iota((span, frames), 1) == frame_in(iota((span, frames), 0) // REACH)), time_wide
    )
    for h in range(halves):
        axial_rows = jnp.broadcast_to(
            axial_wide[h * REACH:(h + 1) * REACH][None], (frames, REACH, wide)
        ).reshape(span, wide)
        forward_mix[h * span:(h + 1) * span] = (axial_rows * time_rows).astype(BF16)

    lane = iota((all_planes, wide), 1)
    spread = hot(
        iota((all_planes, wide), 0) == plane_at(lane // span * REACH + lane % REACH)
    )
    pick = hot(iota((planes, all_planes), 1) == first + iota((planes, all_planes), 0))
    axial_wide = exact(exact_nt(pick, axial[...]), spread)
    same = hot(iota((frames, frames), 0) == iota((frames, frames), 1))
    time_wide = exact(
        exact_nt(same, temporal[...]),
        hot(iota((frames, wide), 0) == frame_in(iota((frames, wide), 1) // REACH % frames)),
    )
    axial_rows = exact(hot(iota((cells, planes), 1) == iota((cells, planes), 0) // frames), axial_wide)
    time_rows = jnp.broadcast_to(time_wide[None], (planes, frames, wide)).reshape(cells, wide)
    backward_mix[...] = (axial_rows * time_rows).astype(BF16)

    def stage_image(c):
        for o in range(1, ways):
            a2a(0, c, o).wait_recv()
        moved = jnp.dot(swap[0], inbox[0, c].reshape(cells, width), preferred_element_type=F32)
        image[c, 1:planes + 1] = moved.astype(BF16).reshape(planes, frames, width)
        halo_start(0, c)

    group = 4

    def slot_of(r, j):
        return chosen[3 * r + j], codes[3 * r + j]

    def weight(code, value):
        return jnp.where(code == value, 1.0, 0.0).astype(F32)

    def stage_forward(c):
        halo_wait(0, c)
        if c == 0:
            local[3].wait()
        image[c, 0] = image_rim[c, LEFT]
        image[c, planes + 1] = image_rim[c, RIGHT]
        for b in range(per_chunk):
            lanes = slice(b * edge, (b + 1) * edge)

            def some_planes(step, carry):
                for u in range(group):
                    z = step * group + u
                    r = z * tiles + c * per_chunk + b
                    near = [image[c, z + d, :, lanes].astype(F32) for d in range(3)]
                    total = None
                    for j in range(3):
                        slot, code = slot_of(r, j)
                        picked = sum(near[d] * weight(code, d + 1) for d in range(3)).astype(BF16)
                        term = lax.dot_general(
                            picked, kernel[slot], (((1,), (1,)), ((), ())),
                            preferred_element_type=F32,
                        )
                        total = term if total is None else total + term
                    at = pl.multiple_of(z * frames, frames)
                    gathered[pl.ds(at, frames), lanes] = total.astype(BF16)
                return carry

            lax.fori_loop(0, planes // group, some_planes, 0)
        coef[c] = gathered[...]
        halo_start(1, c)

    def by_half(box, c, h):
        cube = box[c].astype(F32).reshape(frames, halves, REACH, width)
        return cube[:, h].reshape(span, width)

    def stage_ratio(c):
        for kind in (1, 2):
            for o in range(1, ways):
                a2a(kind, c, o).wait_recv()
        projected = jnp.dot(forward_mix[:, :cells], coef[c], preferred_element_type=F32)
        halo_wait(1, c)
        projected = projected + jnp.dot(
            forward_mix[:, cells:], coef_rim[c].reshape(2 * span, width), preferred_element_type=F32
        )
        for h in range(halves):
            expected = projected[h * span:(h + 1) * span] + by_half(inbox.at[2], c, h)
            ratio[c, h * span:(h + 1) * span] = (
                by_half(inbox.at[1], c, h) / expected
            ).astype(BF16)
        halo_start(2, c)

    def stage_back(c):
        mixed = jnp.dot(backward_mix[:, :cells], ratio[c], preferred_element_type=F32)
        halo_wait(2, c)
        mixed = mixed + jnp.dot(
            backward_mix[:, cells:], ratio_rim[c].reshape(2 * span, width), preferred_element_type=F32
        )
        low[c] = mixed.astype(BF16).reshape(planes, frames, width)
        back[c] = jnp.zeros((planes + 2, frames, width), F32)
        for b in range(per_chunk):
            lanes = slice(b * edge, (b + 1) * edge)

            def some_planes(step, carry):
                sums = [jnp.zeros((frames, edge), F32) for _ in range(group + 2)]
                for u in range(group):
                    z = step * group + u
                    r = z * tiles + c * per_chunk + b
                    values = low[c, z, :, lanes]
                    for j in range(3):
                        slot, code = slot_of(r, j)
                        term = jnp.dot(values, kernel[slot], preferred_element_type=F32)
                        for d in range(3):
                            sums[u + d] = sums[u + d] + term * weight(code, d + 1)
                for u in range(group + 2):
                    back[c, step * group + u, :, lanes] += sums[u]
                return carry

            lax.fori_loop(0, planes // group, some_planes, 0)
        rim_out[c, LEFT] = back[c, 0]
        rim_out[c, RIGHT] = back[c, planes + 1]
        halo_start(3, c)

    def stage_send(c):
        halo_wait(3, c)
        back[c, 1] += rim[c, 0]
        back[c, planes] += rim[c, 1]
        whole = back[c, 1:planes + 1].reshape(cells, width)
        high = whole.astype(BF16)
        rest = (whole - high.astype(F32)).astype(BF16)
        moved = jnp.dot(swap[1], high, preferred_element_type=F32) + jnp.dot(
            swap[1], rest, preferred_element_type=F32
        )
        moved = moved.reshape(ways, own * planes, width)
        final_out[c] = moved
        for o in range(1, ways):
            a2a(3, c, o).start()

    def stage_out(c):
        if c == 0:
            local[4].wait()
        for o in range(ways):
            if o > 0:
                a2a(3, c, o).wait_recv()
            source = lax.rem(me + ways - o, ways)
            lanes = pl.ds(pl.multiple_of(source * tile + c * width, edge), width)
            values = (final_in if o else final_out)[c, o].reshape(own, planes, width)
            out[:, :, lanes] = alpha[:, :, lanes] * values / norm[:, :, lanes]

    stages = (stage_image, stage_forward, stage_ratio, stage_back, stage_send, stage_out)
    for t in range(CHUNKS + len(stages) - 1):
        for s, stage in enumerate(stages):
            if 0 <= t - s < CHUNKS:
                stage(t - s)

    for c in range(CHUNKS):
        for kind in range(4):
            for o in range(1, ways):
                a2a(kind, c, o).wait_send()
            for side in (LEFT, RIGHT):
                halo(kind, c, side).wait_send()


def on_device(alpha, measured, background, norm_image, temporal, axial, kernel, rows, cols, counts):
    own, planes, row_width = alpha.shape
    ways, slabs = lax.axis_size("frame"), lax.axis_size("zslab")
    slots, edge, _ = kernel.shape
    frames = ways * own
    tile = row_width // ways
    width = tile // CHUNKS
    cells = planes * frames
    wide = (planes + 2 * REACH) * frames
    tiles_all, tiles = row_width // edge, tile // edge
    first = lax.axis_index("zslab") * planes
    here = lax.axis_index("frame") * tiles
    local_rows = (rows // tiles_all - first) * tiles + rows % tiles_all - here
    step = cols // tiles_all - rows // tiles_all
    live = jnp.arange(slots, dtype=I32) < counts[0]
    local_rows = jnp.where(live, local_rows, planes * tiles)
    order = jnp.arange(planes * tiles, dtype=I32)
    starts = jnp.sum((local_rows[None, :] < order[:, None]).astype(I32), axis=1)
    places = starts[:, None] + jnp.arange(3, dtype=I32)[None, :]
    chosen = places[:, :, None] == jnp.arange(slots, dtype=I32)[None, None, :]
    mine = chosen & (local_rows[None, None, :] == order[:, None, None])
    codes = jnp.sum(jnp.where(mine, step + 2, 0), axis=2).reshape(-1)
    spots = jnp.minimum(places, slots - 1).reshape(-1)
    sizes = (ways, slabs, own, planes, tile, slots)
    hbm = pl.BlockSpec(memory_space=pl.ANY)
    vmem = pl.BlockSpec(memory_space=pltpu.VMEM)
    smem = pl.BlockSpec(memory_space=pltpu.SMEM)
    box = (CHUNKS, ways, own * planes, width)
    return pl.pallas_call(
        functools.partial(em_kernel, sizes),
        out_shape=jax.ShapeDtypeStruct(alpha.shape, F32),
        in_specs=[hbm] * 4 + [vmem] * 2 + [hbm] + [smem] * 2,
        out_specs=vmem,
        scratch_shapes=[pltpu.VMEM(alpha.shape, F32)] * 4 + [
            pltpu.VMEM(kernel.shape, BF16),
            pltpu.VMEM((3, CHUNKS, ways - 1, own * planes, width), BF16),
            pltpu.VMEM((3,) + box, BF16),
            pltpu.VMEM((CHUNKS, planes + 2, frames, width), BF16),
            pltpu.VMEM((CHUNKS, cells, width), BF16),
            pltpu.VMEM((CHUNKS, cells, width), BF16),
            pltpu.VMEM((CHUNKS, 2, frames, width), BF16),
            pltpu.VMEM((CHUNKS, 2, REACH * frames, width), BF16),
            pltpu.VMEM((CHUNKS, 2, REACH * frames, width), BF16),
            pltpu.VMEM((CHUNKS, planes, frames, width), BF16),
            pltpu.VMEM((CHUNKS, planes + 2, frames, width), F32),
            pltpu.VMEM((CHUNKS, 2, frames, width), F32),
            pltpu.VMEM((CHUNKS, 2, frames, width), F32),
            pltpu.VMEM(box, F32),
            pltpu.VMEM(box, F32),
            pltpu.VMEM((cells, width), BF16),
            pltpu.VMEM((2, cells, cells), BF16),
            pltpu.VMEM((cells, wide), BF16),
            pltpu.VMEM((cells, wide), BF16),
            pltpu.SemaphoreType.DMA((4, CHUNKS, ways - 1)),
            pltpu.SemaphoreType.DMA((4, CHUNKS, ways - 1)),
            pltpu.SemaphoreType.DMA((4, CHUNKS, 2)),
            pltpu.SemaphoreType.DMA((4, CHUNKS, 2)),
            pltpu.SemaphoreType.DMA((5,)),
        ],
        compiler_params=pltpu.CompilerParams(
            collective_id=0, has_side_effects=True, vmem_limit_bytes=48 * 1024 * 1024
        ),
        cost_estimate=pl.CostEstimate(
            flops=8 * frames * slots * edge * edge, bytes_accessed=2 * slots * edge * edge,
            transcendentals=0,
        ),
    )(alpha, measured, background, norm_image, temporal, axial, kernel, codes, spots)


def solution(mesh):
    placed = (
        P(("study", "frame"), "zslab", None),
        P(("study", "frame"), "zslab", None),
        P(("study", "frame"), "zslab", None),
        P(("study", "frame"), "zslab", None),
        P(),
        P(),
        P(("study", "zslab", "frame"), None, None),
        P(("study", "zslab", "frame")),
        P(("study", "zslab", "frame")),
        P(("study", "zslab", "frame")),
    )
    return jax.shard_map(
        on_device,
        mesh=mesh,
        in_specs=placed,
        out_specs=P(("study", "frame"), "zslab", None),
        check_vma=False,
    )
```
